32 devices in a mesh: tile: 16 (over z, y, core), grp: 2 (over x).
Axes of the slice: x: 2, y: 2, z: 4, core: 2. Of those that a mesh axis runs over, the one named last changes fastest.
Arguments:
- points: bfloat16 [4096, 256], P(('tile', 'grp')), may hold values from -6 to 6
- targets: bfloat16 [4096], P(('tile', 'grp')), may hold values from -12 to 12
- morton: int32 [4096], P(('tile', 'grp')), may hold values from 0 to 15, as said below
- inducing: bfloat16 [8192, 256], P('tile'), may hold values from -6 to 6
- means: bfloat16 [8192], P('tile'), may hold values from -6 to 6
- scales: bfloat16 [8192], P('tile'), may hold values from 0.099609375 to 1.3984375
- neighbours: int32 [16, 8], replicated, may hold values from 0 to 63, as said below
Outputs:
- grad_inducing: float32 [8192, 256], P(('tile', 'grp'))
- grad_means: float32 [8192], P(('tile', 'grp'))
- grad_scales: float32 [8192], P(('tile', 'grp'))
The draws below stay inside these ranges and needn't reach their ends.
Inputs may be any that keep to these rules, and one draw needn't show every extreme that they name: `morton`: each aligned block of 128 rows names every tile exactly 8 times. `neighbours`: block b is owned by tile b // 4. Row t names only blocks owned by tiles t - 1, t and t + 1; entry 0 is owned by tile t - 1 and entry 1 by tile t + 1 where these exist (else by t), entry 2 by t. Ids may repeat.
All inputs are finite; a program needn't handle non-finite values.
Results may differ from the reference program's by a relative error of at most 0.0003.
Values may be sent and summed in bfloat16 or wider, within the bound.
A program may use at most 64 MiB of HBM per device.

```python
import math
import jax
import jax.numpy as jnp
from jax import lax

F = 256
BS = 128
BLK_DEV = 4
K_NB = 8
PER = 8
ROWS = 128
NPTS = 4096
NBLK = 64
INDUCING = 8192
N_TILE = 16
N_GRP = 2


def draw_morton(key, part):
    shards = NPTS // ROWS
    base = jnp.tile(jnp.arange(N_TILE, dtype=jnp.int32), PER)
    keys = jax.random.split(jax.random.fold_in(key, 3), shards)

    def shuffle(sub_key):
        return jax.random.permutation(sub_key, base)
    return jax.vmap(shuffle)(keys).reshape(-1).astype(jnp.int32)


def draw_neighbours(key, part):
    first_key, second_key = jax.random.split(jax.random.fold_in(key, 7))
    offsets = jax.random.randint(first_key, (N_TILE, K_NB), -1, 2).astype(jnp.int32)
    offsets = offsets.at[:, 0].set(-1).at[:, 1].set(1).at[:, 2].set(0)
    tile_ids = jnp.arange(N_TILE, dtype=jnp.int32)[:, None]
    owner = jnp.clip(tile_ids + offsets, 0, N_TILE - 1)
    local = jax.random.randint(second_key, (N_TILE, K_NB), 0, BLK_DEV).astype(jnp.int32)
    local = local.at[0, 2].set(0).at[N_TILE - 1, 2].set(BLK_DEV - 1)
    return (owner * BLK_DEV + local).astype(jnp.int32)


def steps_of(own_key, shape, cuts, low, high):
    level = 1.0
    for axis_at, shards_of in cuts:
        steps = jax.random.uniform(jax.random.fold_in(jax.random.fold_in(own_key, 6), axis_at), (shards_of,), jnp.float32, low / len(cuts), high / len(cuts))
        level = level * jnp.repeat(jnp.exp(steps), shape[axis_at] // shards_of).reshape((-1,) + (1,) * (len(shape) - 1 - axis_at))
    return level


def centred(stream_key, shape, spread, reach, cuts=(), kind=jnp.bfloat16):
    loudness = steps_of(stream_key, shape, cuts, -0.22, 0.18) if cuts else 1.0
    array = jax.random.normal(stream_key, shape, jnp.float32) * spread * loudness
    return jnp.minimum(jnp.maximum(array, -reach), reach).astype(kind)


def setup_inputs(seed: int = 0) -> dict:
    seeds = jax.random.split(jax.random.key(seed), 8)
    points = centred(seeds[0], (NPTS, F), 1.0, 6.0, ((0, 32),))
    targets = centred(seeds[1], (NPTS,), 2.0, 12.0, ((0, 32),))
    morton = draw_morton(jax.random.fold_in(seeds[7], 71), 0)
    inducing = centred(seeds[3], (INDUCING, F), 1.0, 6.0, ((0, 16),))
    means = centred(seeds[4], (INDUCING,), 1.0, 6.0, ((0, 16),))
    scales = jnp.clip(jnp.exp(math.log(1.3984375) - 2.6418545 * jax.random.uniform(seeds[5], (INDUCING,), jnp.float32) ** steps_of(seeds[5], (INDUCING,), ((0, 16),), -0.2, 0.2)), 0.099609375, 1.3984375).astype(jnp.bfloat16)
    neighbours = draw_neighbours(jax.random.fold_in(seeds[7], 71), 0)
    return {"points": points, "targets": targets, "morton": morton, "inducing": inducing, "means": means, "scales": scales, "neighbours": neighbours}


def kernel_block(feats, feat_sq, block_rows, block_scale):
    cross = lax.dot_general(feats, block_rows, (((1,), (1,)), ((), ())), preferred_element_type=jnp.float32)
    block_f = block_rows.astype(jnp.float32)
    block_sq = lax.optimization_barrier(jnp.sum(block_f * block_f, axis=1))
    dist_sq = feat_sq[:, None] + block_sq[None, :] - 2.0 * cross
    radius = jnp.sqrt(block_scale[None, :] * dist_sq / (2.0 * F))
    remain = 1.0 - jnp.minimum(radius, 1.0)
    value = remain ** 4 * (4.0 * radius + 1.0)
    slope = -10.0 * remain ** 3
    return (value, slope, dist_sq, block_f)

def reference(points, targets, morton, inducing, means, scales, neighbours):
    count = ROWS * N_GRP
    order = jnp.argsort(morton, stable=True)
    feats_all = jnp.take(points, order, axis=0).reshape(N_TILE, count, F)
    wanted_all = jnp.take(targets, order, axis=0).astype(jnp.float32).reshape(N_TILE, count)
    blocks = inducing.reshape(NBLK, BS, F)
    mean_all = means.astype(jnp.float32).reshape(NBLK, BS)
    scale_all = scales.astype(jnp.float32).reshape(NBLK, BS)

    def visit(carry, item):
        grad_rows, grad_mean, grad_scale = carry
        feats, wanted, block_ids = item
        feats_f = feats.astype(jnp.float32)
        feat_sq = lax.optimization_barrier(jnp.sum(feats_f * feats_f, axis=1))
        estimate = jnp.zeros((count,), jnp.float32)
        for slot in range(K_NB):
            value, slope, dist_sq, block_f = kernel_block(feats, feat_sq, blocks[block_ids[slot]], scale_all[block_ids[slot]])
            estimate = estimate + jnp.dot(value, mean_all[block_ids[slot]], precision=lax.Precision.HIGHEST)
        error = estimate - wanted
        for slot in range(K_NB):
            block = block_ids[slot]
            block_scale = scale_all[block]
            value, slope, dist_sq, block_f = kernel_block(feats, feat_sq, blocks[block], block_scale)
            weight = error[:, None] * mean_all[block][None, :] * slope
            mean_piece = jnp.dot(error, value, precision=lax.Precision.HIGHEST)
            scale_piece = lax.optimization_barrier(jnp.sum(weight * dist_sq, axis=0)) / (2.0 * F)
            column = lax.optimization_barrier(jnp.sum(weight, axis=0))
            back = lax.dot_general(weight.astype(jnp.bfloat16), feats, (((0,), (0,)), ((), ())), preferred_element_type=jnp.float32)
            row_piece = (block_scale / F)[:, None] * (block_f * column[:, None] - back)
            grad_rows = grad_rows.at[block].add(row_piece)
            grad_mean = grad_mean.at[block].add(mean_piece)
            grad_scale = grad_scale.at[block].add(scale_piece)
        return ((grad_rows, grad_mean, grad_scale), None)
    start = (jnp.zeros((NBLK, BS, F), jnp.float32), jnp.zeros((NBLK, BS), jnp.float32), jnp.zeros((NBLK, BS), jnp.float32))
    (grad_rows, grad_mean, grad_scale), unused = lax.scan(visit, start, (feats_all, wanted_all, neighbours))
    norm = 1.0 / jnp.sqrt(jnp.float32(count))
    return (grad_rows.reshape(INDUCING, F) * norm, grad_mean.reshape(INDUCING) * norm, grad_scale.reshape(INDUCING) * norm)
```

```python
import functools
import math

import jax
import jax.numpy as jnp
from jax import lax
from jax.experimental import pallas as pl
from jax.experimental.pallas import tpu as pltpu
from jax.sharding import PartitionSpec as P

BS = 128
LANES = 128
F32 = jnp.float32
BF16 = jnp.bfloat16
MESH = pl.DeviceIdType.MESH
NT = (((1,), (1,)), ((), ()))


def iota(shape, dim):
    return lax.broadcasted_iota(jnp.int32, shape, dim)


def repeat(count, body):
    if count <= 16:
        for index in range(count):
            body(index)
    else:
        lax.fori_loop(0, count, lambda index, carry: (body(index), carry)[1], 0)


def to_column(row):
    eye = iota((LANES, LANES), 0) == iota((LANES, LANES), 1)
    return jnp.sum(jnp.where(eye, row, 0.0), axis=1, keepdims=True)


def to_row(column):
    eye = iota((LANES, LANES), 0) == iota((LANES, LANES), 1)
    return jnp.sum(jnp.where(eye, column, 0.0), axis=0, keepdims=True)


def kernel(
    tiles, groups,
    points, targets, morton, inducing, means, scales, neighbours,
    grad_rows, grad_means, grad_scales,
    grouped, landed, feats, mine_part, parts, dist, value, slope, errors,
    send1, recv1, send2, recv2, send3, recv3,
):
    rows, width = points.shape
    per = rows // tiles
    owned = means.shape[0]
    mine = owned // groups
    size = mine * BS
    count = neighbours.shape[1]
    chunks = rows // LANES
    here = lax.axis_index("tile")
    grp = lax.axis_index("grp")

    def exists(tile):
        return (tile >= 0) & (tile < tiles)

    def other(step):
        return lax.rem(grp + step, groups)

    def source(step):
        return lax.rem(grp + groups - step, groups)

    barrier = pltpu.get_barrier_semaphore()

    def greet(step):
        pl.semaphore_signal(
            barrier, inc=1,
            device_id=(lax.rem(here + step + 1, tiles), grp), device_id_type=MESH,
        )

    repeat(tiles - 1, greet)
    expected = jnp.int32(tiles - 1)
    for d in range(-2, 3):
        there = exists(here + d)
        expected += jnp.where(there, groups - 1, 0)

        @pl.when(there)
        def _():
            for step in range(1, groups):
                pl.semaphore_signal(
                    barrier, inc=1, device_id=(here + d, other(step)), device_id_type=MESH
                )

        if d:
            @pl.when(jnp.logical_not(there))
            def _():
                parts[d + 2] = jnp.zeros(parts.shape[1:], F32)
                if abs(d) == 1:
                    feats[d + 1] = jnp.zeros(feats.shape[1:], BF16)

    codes = morton[...]
    member = iota((tiles, rows), 0) == codes
    before = jnp.dot(
        member.astype(F32).astype(BF16),
        (iota((rows, rows), 0) < iota((rows, rows), 1)).astype(F32).astype(BF16),
        preferred_element_type=F32,
    )
    rank = jnp.sum(jnp.where(member, before, 0.0), axis=0, keepdims=True)
    place = codes * per + rank.astype(jnp.int32)
    chosen = iota((rows, rows), 0) == place
    moved = jnp.dot(
        chosen.astype(F32).astype(BF16), points[...], preferred_element_type=F32
    )
    goals = jnp.sum(jnp.where(chosen, targets[...].astype(F32), 0.0), axis=1, keepdims=True)
    grouped[:, :, :width] = moved.reshape(tiles, per, width).astype(BF16)
    grouped[:, :, width:] = (
        jnp.broadcast_to(goals, (rows, LANES)).reshape(tiles, per, LANES).astype(BF16)
    )
    pl.semaphore_wait(barrier, expected)

    def first(step):
        to = lax.rem(here + step + 1, tiles)
        return pltpu.make_async_remote_copy(
            src_ref=grouped.at[to], dst_ref=landed.at[here],
            send_sem=send1.at[step], recv_sem=recv1.at[step],
            device_id=(to, grp), device_id_type=MESH,
        )

    repeat(tiles - 1, lambda step: first(step).start())
    landed[here] = grouped[here]

    own = inducing[pl.ds(pl.multiple_of(grp * size, size), size), :]
    own_f = own.astype(F32)
    own_sq = jnp.sum(own_f * own_f, axis=1, keepdims=True)

    def own_column(ref):
        every = ref[...].astype(F32)
        picked = [
            to_column(jnp.sum(
                jnp.where(iota(every.shape, 0) == grp * mine + b, every, 0.0),
                axis=0, keepdims=True,
            ))
            for b in range(mine)
        ]
        return jnp.concatenate(picked, axis=0)

    mean = own_column(means)
    scale = own_column(scales)
    scaled = scale / (2.0 * width)
    times = []
    for r in range(3):
        tile = here + r - 1
        row = jnp.clip(tile, 0, tiles - 1)
        pieces = []
        for b in range(mine):
            block = here * owned + grp * mine + b
            listed = jnp.int32(0)
            for k in range(count):
                listed += jnp.where(neighbours[row, k] == block, 1, 0)
            listed = jnp.where(exists(tile), listed, 0)
            pieces.append(jnp.full((BS, 1), listed.astype(F32), F32))
        times.append(jnp.concatenate(pieces, axis=0))

    repeat(tiles - 1, lambda step: first(step).wait_recv())
    arrived = landed[...].astype(F32).reshape(rows, width + LANES)
    feats[1, grp] = arrived[:, :width].astype(BF16)

    def second(d, step):
        return pltpu.make_async_remote_copy(
            src_ref=feats.at[1, grp], dst_ref=feats.at[1 - d, grp],
            send_sem=send2.at[1 - d, step], recv_sem=recv2.at[1 - d, step],
            device_id=(here + d, other(step)), device_id_type=MESH,
        )

    hops = [(d, s) for d in (1, -1, 0) for s in range(groups) if (d, s) != (0, 0)]
    for d, s in hops:
        @pl.when(exists(here + d))
        def _():
            second(d, s).start()

    ones = jnp.ones((8, width), BF16)

    def forward(r, group):
        def piece(c):
            span = pl.ds(pl.multiple_of(c * LANES, LANES), LANES)
            block = feats[r, group, span, :]
            block_f = block.astype(F32)
            square = block_f * block_f
            high = square.astype(BF16)
            low = (square - high.astype(F32)).astype(BF16)
            feat_sq = (
                lax.dot_general(ones, high, NT, preferred_element_type=F32)
                + lax.dot_general(ones, low, NT, preferred_element_type=F32)
            )[:1]
            cross = lax.dot_general(own, block, NT, preferred_element_type=F32)
            far = (feat_sq + own_sq) - 2.0 * cross
            radius = jnp.sqrt(jnp.maximum(scaled * far, 0.0))
            remain = 1.0 - jnp.minimum(radius, 1.0)
            square_r = remain * remain
            height = square_r * square_r * (4.0 * radius + 1.0)
            dist[r, group, :, span] = far
            value[r, group, :, span] = height
            slope[r, group, :, span] = -10.0 * (square_r * remain)
            mine_part[r, group, :, span] = jnp.sum(
                (mean * times[r]) * height, axis=0, keepdims=True
            )

        repeat(chunks, piece)

    forward(1, grp)
    for c in range(chunks):
        span = pl.ds(c * LANES, LANES)
        goal = to_row(arrived[c * LANES:(c + 1) * LANES, width:])
        mine_part[1, grp, :, span] = mine_part[1, grp, :, span] - goal

    order = [(r, s) for r in (1, 0, 2) for s in range(groups) if (r, s) != (1, 0)]
    for r, s in order:
        @pl.when(exists(here + r - 1))
        def _():
            second(1 - r, s).wait_recv()

        forward(r, source(s))

    def third(d, step):
        return pltpu.make_async_remote_copy(
            src_ref=mine_part, dst_ref=parts.at[2 - d, grp],
            send_sem=send3.at[2 - d, step], recv_sem=recv3.at[2 - d, step],
            device_id=(here + d, other(step)), device_id_type=MESH,
        )

    spread = [(d, s) for d in range(-2, 3) for s in range(groups) if (d, s) != (0, 0)]
    for d, s in spread:
        @pl.when(exists(here + d))
        def _():
            third(d, s).start()

    parts[2, grp] = mine_part[...]
    for d, s in spread:
        @pl.when(exists(here - d))
        def _():
            third(d, s).wait_recv()

    total_mean = jnp.zeros((size, 1), F32)
    total_scale = jnp.zeros((size, 1), F32)
    total_column = jnp.zeros((size, 1), F32)
    total_back = jnp.zeros((size, width), F32)
    for r in range(3):
        for group in range(groups):
            error = jnp.zeros((1, rows), F32)
            for d in range(r - 2, r + 1):
                for sender in range(groups):
                    error = error + parts[d + 2, sender, r - d, group]
            errors[group] = error

        def backward(index, carry):
            sum_mean, sum_scale, sum_column, back = carry
            group, c = index // chunks, lax.rem(index, chunks)
            span = pl.ds(pl.multiple_of(c * LANES, LANES), LANES)
            error = errors[group, :, span]
            weight = (error * mean) * slope[r, group, :, span]
            sum_mean = sum_mean + error * value[r, group, :, span]
            sum_scale = sum_scale + weight * dist[r, group, :, span]
            sum_column = sum_column + weight
            back = back + jnp.dot(
                weight.astype(BF16), feats[r, group, span, :], preferred_element_type=F32
            )
            return sum_mean, sum_scale, sum_column, back

        flat = jnp.zeros((size, LANES), F32)
        carry = (flat, flat, flat, jnp.zeros((size, width), F32))
        if groups * chunks <= 4:
            for index in range(groups * chunks):
                carry = backward(jnp.int32(index), carry)
        else:
            carry = lax.fori_loop(0, groups * chunks, backward, carry)
        total_mean += times[r] * jnp.sum(carry[0], axis=1, keepdims=True)
        total_scale += times[r] * jnp.sum(carry[1], axis=1, keepdims=True)
        total_column += times[r] * jnp.sum(carry[2], axis=1, keepdims=True)
        total_back += times[r] * carry[3]

    norm = 1.0 / math.sqrt(rows * groups)
    grad_rows[...] = (scale * (norm / width)) * (own_f * total_column - total_back)
    for b in range(mine):
        at = slice(b * BS, (b + 1) * BS)
        grad_means[:, at] = to_row(total_mean[at]) * norm
        grad_scales[:, at] = to_row(total_scale[at]) * (norm / (2.0 * width))

    repeat(tiles - 1, lambda step: first(step).wait_send())
    for d, s in hops:
        @pl.when(exists(here + d))
        def _():
            second(d, s).wait_send()
    for d, s in spread:
        @pl.when(exists(here + d))
        def _():
            third(d, s).wait_send()


def shards(points, targets, morton, inducing, means, scales, neighbours):
    tiles = lax.axis_size("tile")
    groups = lax.axis_size("grp")
    rows, width = points.shape
    per = rows // tiles
    owned = inducing.shape[0] // BS
    size = owned // groups * BS
    vmem = pl.BlockSpec(memory_space=pltpu.VMEM)
    dma = pltpu.SemaphoreType.DMA
    pair = (3, groups, size, rows)
    result = pl.pallas_call(
        functools.partial(kernel, tiles, groups),
        out_shape=(
            jax.ShapeDtypeStruct((size, width), F32),
            jax.ShapeDtypeStruct((1, size), F32),
            jax.ShapeDtypeStruct((1, size), F32),
        ),
        in_specs=[vmem] * 6 + [pl.BlockSpec(memory_space=pltpu.SMEM)],
        out_specs=(vmem, vmem, vmem),
        scratch_shapes=[
            pltpu.VMEM((tiles, per, width + LANES), BF16),
            pltpu.VMEM((tiles, per, width + LANES), BF16),
            pltpu.VMEM((3, groups, rows, width), BF16),
            pltpu.VMEM((3, groups, 1, rows), F32),
            pltpu.VMEM((5, groups, 3, groups, 1, rows), F32),
            pltpu.VMEM(pair, F32),
            pltpu.VMEM(pair, F32),
            pltpu.VMEM(pair, F32),
            pltpu.VMEM((groups, 1, rows), F32),
            dma((tiles - 1,)), dma((tiles - 1,)),
            dma((3, groups)), dma((3, groups)),
            dma((5, groups)), dma((5, groups)),
        ],
        compiler_params=pltpu.CompilerParams(
            collective_id=0, has_side_effects=True, vmem_limit_bytes=48 << 20
        ),
    )(
        points, targets.reshape(1, rows), morton.reshape(1, rows), inducing,
        means.reshape(owned, BS), scales.reshape(owned, BS), neighbours,
    )
    return result[0], result[1].reshape(size), result[2].reshape(size)


def solution(mesh):
    placed = (
        P(("tile", "grp"), None),
        P(("tile", "grp")),
        P(("tile", "grp")),
        P("tile", None),
        P("tile"),
        P("tile"),
        P(),
    )
    return jax.shard_map(
        shards,
        mesh=mesh,
        in_specs=placed,
        out_specs=(P(("tile", "grp"), None), P(("tile", "grp")), P(("tile", "grp"))),
        check_vma=False,
    )
```

```python
import functools
import math

import jax
import jax.numpy as jnp
from jax import lax
from jax.experimental import pallas as pl
from jax.experimental.pallas import tpu as pltpu
from jax.sharding import PartitionSpec as P

BS = 128
LANES = 128
F32 = jnp.float32
BF16 = jnp.bfloat16
MESH = pl.DeviceIdType.MESH
NT = (((1,), (1,)), ((), ()))


def iota(shape, dim):
    return lax.broadcasted_iota(jnp.int32, shape, dim)


def repeat(count, body):
    if count <= 16:
        for index in range(count):
            body(index)
    else:
        lax.fori_loop(0, count, lambda index, carry: (body(index), carry)[1], 0)


def to_column(row):
    eye = iota((LANES, LANES), 0) == iota((LANES, LANES), 1)
    return jnp.sum(jnp.where(eye, row, 0.0), axis=1, keepdims=True)


def to_row(column):
    eye = iota((LANES, LANES), 0) == iota((LANES, LANES), 1)
    return jnp.sum(jnp.where(eye, column, 0.0), axis=0, keepdims=True)


def kernel(
    tiles, groups,
    points_in, targets_in, morton_in, inducing_in, means_in, scales_in, neighbours_in,
    grad_rows, grad_means, grad_scales,
    points, targets, morton, inducing, means, scales, neighbours, loads,
    grouped, landed, feats, mine_part, parts, dist, value, slope, errors,
    send1, recv1, send2, recv2, send3, recv3,
):
    rows, width = points.shape
    per = rows // tiles
    owned = means.shape[0]
    mine = owned // groups
    size = mine * BS
    count = neighbours.shape[0]
    chunks = rows // LANES
    here = lax.axis_index("tile")
    grp = lax.axis_index("grp")

    own_rows = pl.ds(pl.multiple_of(grp * size, size), size)
    pairs = (
        (morton_in, morton), (points_in, points), (targets_in, targets),
        (inducing_in.at[own_rows, :], inducing), (means_in, means),
        (scales_in, scales), (neighbours_in, neighbours),
    )
    load = [
        pltpu.make_async_copy(pair[0], pair[1], loads.at[index])
        for index, pair in enumerate(pairs)
    ]
    for copy in load[:2]:
        copy.start()

    def exists(tile):
        return (tile >= 0) & (tile < tiles)

    def other(step):
        return lax.rem(grp + step, groups)

    def source(step):
        return lax.rem(grp + groups - step, groups)

    barrier = pltpu.get_barrier_semaphore()

    def greet(step):
        pl.semaphore_signal(
            barrier, inc=1,
            device_id=(lax.rem(here + step + 1, tiles), grp), device_id_type=MESH,
        )

    repeat(tiles - 1, greet)
    for copy in load[2:]:
        copy.start()
    expected = jnp.int32(tiles - 1)
    for d in range(-2, 3):
        there = exists(here + d)
        expected += jnp.where(there, groups - 1, 0)

        @pl.when(there)
        def _():
            for step in range(1, groups):
                pl.semaphore_signal(
                    barrier, inc=1, device_id=(here + d, other(step)), device_id_type=MESH
                )

        if d:
            @pl.when(jnp.logical_not(there))
            def _():
                parts[d + 2] = jnp.zeros(parts.shape[1:], F32)
                if abs(d) == 1:
                    feats[d + 1] = jnp.zeros(feats.shape[1:], BF16)

    for copy in load[:3]:
        copy.wait()

    codes = morton[...]
    member = iota((tiles, rows), 0) == codes
    before = jnp.dot(
        member.astype(F32).astype(BF16),
        (iota((rows, rows), 0) < iota((rows, rows), 1)).astype(F32).astype(BF16),
        preferred_element_type=F32,
    )
    rank = jnp.sum(jnp.where(member, before, 0.0), axis=0, keepdims=True)
    place = codes * per + rank.astype(jnp.int32)
    chosen = iota((rows, rows), 0) == place
    moved = jnp.dot(
        chosen.astype(F32).astype(BF16), points[...], preferred_element_type=F32
    )
    goals = jnp.sum(jnp.where(chosen, targets[...].astype(F32), 0.0), axis=1, keepdims=True)
    grouped[:, :, :width] = moved.reshape(tiles, per, width).astype(BF16)
    grouped[:, :, width:] = (
        jnp.broadcast_to(goals, (rows, LANES)).reshape(tiles, per, LANES).astype(BF16)
    )
    pl.semaphore_wait(barrier, expected)

    def first(step):
        to = lax.rem(here + step + 1, tiles)
        return pltpu.make_async_remote_copy(
            src_ref=grouped.at[to], dst_ref=landed.at[here],
            send_sem=send1.at[step], recv_sem=recv1.at[step],
            device_id=(to, grp), device_id_type=MESH,
        )

    repeat(tiles - 1, lambda step: first(step).start())
    landed[here] = grouped[here]

    for copy in load[3:]:
        copy.wait()
    own = inducing[...]
    own_f = own.astype(F32)
    own_sq = jnp.sum(own_f * own_f, axis=1, keepdims=True)

    def own_column(ref):
        every = ref[...].astype(F32)
        picked = [
            to_column(jnp.sum(
                jnp.where(iota(every.shape, 0) == grp * mine + b, every, 0.0),
                axis=0, keepdims=True,
            ))
            for b in range(mine)
        ]
        return jnp.concatenate(picked, axis=0)

    mean = own_column(means)
    scale = own_column(scales)
    scaled = scale / (2.0 * width)
    times = []
    for r in range(3):
        tile = here + r - 1
        row = jnp.clip(tile, 0, tiles - 1)
        pieces = []
        for b in range(mine):
            block = here * owned + grp * mine + b
            listed = jnp.int32(0)
            for k in range(count):
                listed += jnp.where(neighbours[k, row] == block, 1, 0)
            listed = jnp.where(exists(tile), listed, 0)
            pieces.append(jnp.full((BS, 1), listed.astype(F32), F32))
        times.append(jnp.concatenate(pieces, axis=0))

    repeat(tiles - 1, lambda step: first(step).wait_recv())
    arrived = landed[...].astype(F32).reshape(rows, width + LANES)
    feats[1, grp] = arrived[:, :width].astype(BF16)

    near = 1 - 2 * lax.rem(here, 2)

    def share(d, step, group, to):
        return pltpu.make_async_remote_copy(
            src_ref=feats.at[1, group], dst_ref=feats.at[1 - d, group],
            send_sem=send2.at[1 - d, step], recv_sem=recv2.at[1 - d, step],
            device_id=(here + d, to), device_id_type=MESH,
        )

    def across(step):
        return share(0, step, grp, other(step))

    def far_copy(step):
        return share(-near, step, grp, other(step))

    def near_copy(step):
        return share(near, step, source(step), grp)

    for s in range(1, groups):
        across(s).start()

    @pl.when(exists(here + near))
    def _():
        near_copy(0).start()

    @pl.when(exists(here - near))
    def _():
        for s in range(groups):
            far_copy(s).start()

    ones = jnp.ones((8, width), BF16)

    def forward(r, group, listed):
        def piece(c):
            span = pl.ds(pl.multiple_of(c * LANES, LANES), LANES)
            block = feats[r, group, span, :]
            block_f = block.astype(F32)
            square = block_f * block_f
            high = square.astype(BF16)
            low = (square - high.astype(F32)).astype(BF16)
            feat_sq = (
                lax.dot_general(ones, high, NT, preferred_element_type=F32)
                + lax.dot_general(ones, low, NT, preferred_element_type=F32)
            )[:1]
            cross = lax.dot_general(own, block, NT, preferred_element_type=F32)
            far = (feat_sq + own_sq) - 2.0 * cross
            radius = jnp.sqrt(jnp.maximum(scaled * far, 0.0))
            remain = 1.0 - jnp.minimum(radius, 1.0)
            square_r = remain * remain
            height = square_r * square_r * (4.0 * radius + 1.0)
            dist[r, group, :, span] = far
            value[r, group, :, span] = height
            slope[r, group, :, span] = -10.0 * (square_r * remain)
            mine_part[r, group, :, span] = jnp.sum(
                (mean * listed) * height, axis=0, keepdims=True
            )

        repeat(chunks, piece)

    forward(1, grp, times[1])
    for c in range(chunks):
        span = pl.ds(c * LANES, LANES)
        goal = to_row(arrived[c * LANES:(c + 1) * LANES, width:])
        mine_part[1, grp, :, span] = mine_part[1, grp, :, span] - goal

    for s in range(1, groups):
        across(s).wait_recv()

        @pl.when(exists(here + near))
        def _():
            near_copy(s).start()

        forward(1, source(s), times[1])

    for side in (near, -near):
        listed = jnp.where(side > 0, times[2], times[0])
        for s in range(groups):
            @pl.when(exists(here + side))
            def _():
                share(-side, s, source(s), grp).wait_recv()

            forward(1 + side, source(s), listed)

    def third(d, step):
        return pltpu.make_async_remote_copy(
            src_ref=mine_part, dst_ref=parts.at[2 - d, grp],
            send_sem=send3.at[2 - d, step], recv_sem=recv3.at[2 - d, step],
            device_id=(here + d, other(step)), device_id_type=MESH,
        )

    spread = [(d, s) for d in range(-2, 3) for s in range(groups) if (d, s) != (0, 0)]
    for d, s in spread:
        @pl.when(exists(here + d))
        def _():
            third(d, s).start()

    parts[2, grp] = mine_part[...]
    for d, s in spread:
        @pl.when(exists(here - d))
        def _():
            third(d, s).wait_recv()

    total_mean = jnp.zeros((size, 1), F32)
    total_scale = jnp.zeros((size, 1), F32)
    total_column = jnp.zeros((size, 1), F32)
    total_back = jnp.zeros((size, width), F32)
    for r in range(3):
        for group in range(groups):
            error = jnp.zeros((1, rows), F32)
            for d in range(r - 2, r + 1):
                for sender in range(groups):
                    error = error + parts[d + 2, sender, r - d, group]
            errors[group] = error

        def backward(index, carry):
            sum_mean, sum_scale, sum_column, back = carry
            group, c = index // chunks, lax.rem(index, chunks)
            span = pl.ds(pl.multiple_of(c * LANES, LANES), LANES)
            error = errors[group, :, span]
            weight = (error * mean) * slope[r, group, :, span]
            sum_mean = sum_mean + error * value[r, group, :, span]
            sum_scale = sum_scale + weight * dist[r, group, :, span]
            sum_column = sum_column + weight
            back = back + jnp.dot(
                weight.astype(BF16), feats[r, group, span, :], preferred_element_type=F32
            )
            return sum_mean, sum_scale, sum_column, back

        flat = jnp.zeros((size, LANES), F32)
        carry = (flat, flat, flat, jnp.zeros((size, width), F32))
        if groups * chunks <= 4:
            for index in range(groups * chunks):
                carry = backward(jnp.int32(index), carry)
        else:
            carry = lax.fori_loop(0, groups * chunks, backward, carry)
        total_mean += times[r] * jnp.sum(carry[0], axis=1, keepdims=True)
        total_scale += times[r] * jnp.sum(carry[1], axis=1, keepdims=True)
        total_column += times[r] * jnp.sum(carry[2], axis=1, keepdims=True)
        total_back += times[r] * carry[3]

    norm = 1.0 / math.sqrt(rows * groups)
    grad_rows[...] = (scale * (norm / width)) * (own_f * total_column - total_back)
    for b in range(mine):
        at = slice(b * BS, (b + 1) * BS)
        grad_means[:, at] = to_row(total_mean[at]) * norm
        grad_scales[:, at] = to_row(total_scale[at]) * (norm / (2.0 * width))

    repeat(tiles - 1, lambda step: first(step).wait_send())
    for s in range(1, groups):
        across(s).wait_send()

    @pl.when(exists(here + near))
    def _():
        for s in range(groups):
            near_copy(s).wait_send()

    @pl.when(exists(here - near))
    def _():
        for s in range(groups):
            far_copy(s).wait_send()

    for d, s in spread:
        @pl.when(exists(here + d))
        def _():
            third(d, s).wait_send()


def finish(rows, means, scales, out_rows, out_means, out_scales):
    out_rows[...] = rows[...]
    out_means[...] = means[...]
    out_scales[...] = scales[...]


def shards(points, targets, morton, inducing, means, scales, neighbours):
    tiles = lax.axis_size("tile")
    groups = lax.axis_size("grp")
    rows, width = points.shape
    per = rows // tiles
    owned = inducing.shape[0] // BS
    size = owned // groups * BS
    vmem = pl.BlockSpec(memory_space=pltpu.VMEM)
    dma = pltpu.SemaphoreType.DMA
    pair = (3, groups, size, rows)
    result = pl.pallas_call(
        functools.partial(kernel, tiles, groups),
        out_shape=(
            jax.ShapeDtypeStruct((size, width), F32),
            jax.ShapeDtypeStruct((1, size), F32),
            jax.ShapeDtypeStruct((1, size), F32),
        ),
        in_specs=[pl.BlockSpec(memory_space=pltpu.HBM)] * 7,
        out_specs=(vmem, vmem, vmem),
        scratch_shapes=[
            pltpu.VMEM((rows, width), BF16),
            pltpu.VMEM((1, rows), BF16),
            pltpu.VMEM((1, rows), jnp.int32),
            pltpu.VMEM((size, width), BF16),
            pltpu.VMEM((owned, BS), BF16),
            pltpu.VMEM((owned, BS), BF16),
            pltpu.SMEM(neighbours.shape[::-1], jnp.int32),
            dma((7,)),
            pltpu.VMEM((tiles, per, width + LANES), BF16),
            pltpu.VMEM((tiles, per, width + LANES), BF16),
            pltpu.VMEM((3, groups, rows, width), BF16),
            pltpu.VMEM((3, groups, 1, rows), F32),
            pltpu.VMEM((5, groups, 3, groups, 1, rows), F32),
            pltpu.VMEM(pair, F32),
            pltpu.VMEM(pair, F32),
            pltpu.VMEM(pair, F32),
            pltpu.VMEM((groups, 1, rows), F32),
            dma((tiles - 1,)), dma((tiles - 1,)),
            dma((3, groups)), dma((3, groups)),
            dma((5, groups)), dma((5, groups)),
        ],
        compiler_params=pltpu.CompilerParams(
            collective_id=0, has_side_effects=True, vmem_limit_bytes=62 << 20
        ),
    )(
        points, targets.reshape(1, rows), morton.reshape(1, rows), inducing,
        means.reshape(owned, BS), scales.reshape(owned, BS), neighbours.T,
    )
    result = pl.pallas_call(
        finish,
        out_shape=[jax.ShapeDtypeStruct(part.shape, F32) for part in result],
        in_specs=[vmem] * 3,
        out_specs=[vmem] * 3,
    )(*result)
    return result[0], result[1].reshape(size), result[2].reshape(size)


def solution(mesh):
    placed = (
        P(("tile", "grp"), None),
        P(("tile", "grp")),
        P(("tile", "grp")),
        P("tile", None),
        P("tile"),
        P("tile"),
        P(),
    )
    return jax.shard_map(
        shards,
        mesh=mesh,
        in_specs=placed,
        out_specs=(P(("tile", "grp"), None), P(("tile", "grp")), P(("tile", "grp"))),
        check_vma=False,
    )
```

```python
import functools
import math

import jax
import jax.numpy as jnp
from jax import lax
from jax.experimental import pallas as pl
from jax.experimental.pallas import tpu as pltpu
from jax.sharding import PartitionSpec as P

BS = 128
LANES = 128
F32 = jnp.float32
BF16 = jnp.bfloat16
MESH = pl.DeviceIdType.MESH
NT = (((1,), (1,)), ((), ()))


def iota(shape, dim):
    return lax.broadcasted_iota(jnp.int32, shape, dim)


def repeat(count, body):
    if count <= 16:
        for index in range(count):
            body(index)
    else:
        lax.fori_loop(0, count, lambda index, carry: (body(index), carry)[1], 0)


def to_column(row):
    eye = iota((LANES, LANES), 0) == iota((LANES, LANES), 1)
    return jnp.sum(jnp.where(eye, row, 0.0), axis=1, keepdims=True)


def to_row(column):
    eye = iota((LANES, LANES), 0) == iota((LANES, LANES), 1)
    return jnp.sum(jnp.where(eye, column, 0.0), axis=0, keepdims=True)


def kernel(
    tiles, groups,
    points_in, targets_in, morton_in, inducing_in, means_in, scales_in, neighbours_in,
    grad_rows, grad_means, grad_scales,
    points, targets, morton, inducing, means, scales, neighbours, loads,
    grouped, landed, feats, mine_part, parts, dist, value, slope, errors,
    send1, recv1, send2, recv2, send3, recv3,
):
    rows, width = points.shape
    per = rows // tiles
    owned = means.shape[0]
    mine = owned // groups
    size = mine * BS
    count = neighbours.shape[0]
    chunks = rows // LANES
    here = lax.axis_index("tile")
    grp = lax.axis_index("grp")

    own_rows = pl.ds(pl.multiple_of(grp * size, size), size)
    pairs = (
        (morton_in, morton), (points_in, points), (targets_in, targets),
        (inducing_in.at[own_rows, :], inducing), (means_in, means),
        (scales_in, scales), (neighbours_in, neighbours),
    )
    load = [
        pltpu.make_async_copy(pair[0], pair[1], loads.at[index])
        for index, pair in enumerate(pairs)
    ]
    for copy in load[:2]:
        copy.start()

    def exists(tile):
        return (tile >= 0) & (tile < tiles)

    def other(step):
        return lax.rem(grp + step, groups)

    def source(step):
        return lax.rem(grp + groups - step, groups)

    barrier = pltpu.get_barrier_semaphore()

    def greet(step):
        pl.semaphore_signal(
            barrier, inc=1,
            device_id=(lax.rem(here + step + 1, tiles), grp), device_id_type=MESH,
        )

    repeat(tiles - 1, greet)
    for copy in load[2:]:
        copy.start()
    expected = jnp.int32(tiles - 1)
    for d in range(-2, 3):
        there = exists(here + d)
        expected += jnp.where(there, groups - 1, 0)

        @pl.when(there)
        def _():
            for step in range(1, groups):
                pl.semaphore_signal(
                    barrier, inc=1, device_id=(here + d, other(step)), device_id_type=MESH
                )

        if d:
            @pl.when(jnp.logical_not(there))
            def _():
                parts[d + 2] = jnp.zeros(parts.shape[1:], F32)
                if abs(d) == 1:
                    feats[d + 1] = jnp.zeros(feats.shape[1:], BF16)

    for copy in load[:3]:
        copy.wait()

    codes = morton[...]
    member = iota((tiles, rows), 0) == codes
    before = jnp.dot(
        member.astype(F32).astype(BF16),
        (iota((rows, rows), 0) < iota((rows, rows), 1)).astype(F32).astype(BF16),
        preferred_element_type=F32,
    )
    rank = jnp.sum(jnp.where(member, before, 0.0), axis=0, keepdims=True)
    place = codes * per + rank.astype(jnp.int32)
    chosen = iota((rows, rows), 0) == place
    moved = jnp.dot(
        chosen.astype(F32).astype(BF16), points[...], preferred_element_type=F32
    )
    goals = jnp.sum(jnp.where(chosen, targets[...].astype(F32), 0.0), axis=1, keepdims=True)
    grouped[:, :, :width] = moved.reshape(tiles, per, width).astype(BF16)
    grouped[:, :, width:] = (
        jnp.broadcast_to(goals, (rows, LANES)).reshape(tiles, per, LANES).astype(BF16)
    )
    pl.semaphore_wait(barrier, expected)

    def first(step):
        to = lax.rem(here + step + 1, tiles)
        return pltpu.make_async_remote_copy(
            src_ref=grouped.at[to], dst_ref=landed.at[here],
            send_sem=send1.at[step], recv_sem=recv1.at[step],
            device_id=(to, grp), device_id_type=MESH,
        )

    repeat(tiles - 1, lambda step: first(step).start())
    landed[here] = grouped[here]

    for copy in load[3:]:
        copy.wait()
    own = inducing[...]
    own_f = own.astype(F32)
    own_sq = jnp.sum(own_f * own_f, axis=1, keepdims=True)

    def own_column(ref):
        every = ref[...].astype(F32)
        picked = [
            to_column(jnp.sum(
                jnp.where(iota(every.shape, 0) == grp * mine + b, every, 0.0),
                axis=0, keepdims=True,
            ))
            for b in range(mine)
        ]
        return jnp.concatenate(picked, axis=0)

    mean = own_column(means)
    scale = own_column(scales)
    scaled = scale / (2.0 * width)
    times = []
    for r in range(3):
        tile = here + r - 1
        row = jnp.clip(tile, 0, tiles - 1)
        pieces = []
        for b in range(mine):
            block = here * owned + grp * mine + b
            listed = jnp.int32(0)
            for k in range(count):
                listed += jnp.where(neighbours[k, row] == block, 1, 0)
            listed = jnp.where(exists(tile), listed, 0)
            pieces.append(jnp.full((BS, 1), listed.astype(F32), F32))
        times.append(jnp.concatenate(pieces, axis=0))

    near = 1 - 2 * lax.rem(here, 2)

    half = tiles // 2
    front = here // half

    def part(k):
        return front if k == 0 else 1 - front

    def share(d, step, group, to, k):
        span = pl.ds(pl.multiple_of(part(k) * (rows // 2), rows // 2), rows // 2)
        return pltpu.make_async_remote_copy(
            src_ref=feats.at[1, group, span, :], dst_ref=feats.at[1 - d, group, span, :],
            send_sem=send2.at[1 - d, step, k], recv_sem=recv2.at[1 - d, step, k],
            device_id=(here + d, to), device_id_type=MESH,
        )

    def across(step, k):
        return share(0, step, grp, other(step), k)

    def far_copy(step, k):
        return share(-near, step, grp, other(step), k)

    def near_copy(step, k):
        return share(near, step, source(step), grp, k)

    for k in range(2):
        def landing(index):
            tile = part(k) * half + index

            @pl.when(tile != here)
            def _():
                first(lax.rem(here - tile - 1 + tiles, tiles)).wait_recv()

        repeat(half, landing)
        mine_half = landed[pl.ds(part(k) * half, half), :, :].astype(F32)
        mine_half = mine_half.reshape(rows // 2, width + LANES)
        span = pl.ds(pl.multiple_of(part(k) * (rows // 2), rows // 2), rows // 2)
        feats[1, grp, span, :] = mine_half[:, :width].astype(BF16)

        for s in range(1, groups):
            across(s, k).start()

        @pl.when(exists(here + near))
        def _():
            near_copy(0, k).start()

        @pl.when(exists(here - near))
        def _():
            for s in range(groups):
                far_copy(s, k).start()

    arrived = landed[:, :, width:].astype(F32).reshape(rows, LANES)
    ones = jnp.ones((8, width), BF16)

    def forward(r, group, listed):
        def piece(c):
            span = pl.ds(pl.multiple_of(c * LANES, LANES), LANES)
            block = feats[r, group, span, :]
            block_f = block.astype(F32)
            square = block_f * block_f
            high = square.astype(BF16)
            low = (square - high.astype(F32)).astype(BF16)
            feat_sq = (
                lax.dot_general(ones, high, NT, preferred_element_type=F32)
                + lax.dot_general(ones, low, NT, preferred_element_type=F32)
            )[:1]
            cross = lax.dot_general(own, block, NT, preferred_element_type=F32)
            far = (feat_sq + own_sq) - 2.0 * cross
            radius = jnp.sqrt(jnp.maximum(scaled * far, 0.0))
            remain = 1.0 - jnp.minimum(radius, 1.0)
            square_r = remain * remain
            height = square_r * square_r * (4.0 * radius + 1.0)
            dist[r, group, :, span] = far
            value[r, group, :, span] = height
            slope[r, group, :, span] = -10.0 * (square_r * remain)
            mine_part[r, group, :, span] = jnp.sum(
                (mean * listed) * height, axis=0, keepdims=True
            )

        repeat(chunks, piece)

    forward(1, grp, times[1])
    for c in range(chunks):
        span = pl.ds(c * LANES, LANES)
        goal = to_row(arrived[c * LANES:(c + 1) * LANES])
        mine_part[1, grp, :, span] = mine_part[1, grp, :, span] - goal

    for s in range(1, groups):
        for k in range(2):
            across(s, k).wait_recv()

            @pl.when(exists(here + near))
            def _():
                near_copy(s, k).start()

        forward(1, source(s), times[1])

    for side in (near, -near):
        listed = jnp.where(side > 0, times[2], times[0])
        for s in range(groups):
            @pl.when(exists(here + side))
            def _():
                for k in range(2):
                    share(-side, s, source(s), grp, k).wait_recv()

            forward(1 + side, source(s), listed)

    def third(d, step):
        return pltpu.make_async_remote_copy(
            src_ref=mine_part, dst_ref=parts.at[2 - d, grp],
            send_sem=send3.at[2 - d, step], recv_sem=recv3.at[2 - d, step],
            device_id=(here + d, other(step)), device_id_type=MESH,
        )

    spread = [(d, s) for d in range(-2, 3) for s in range(groups) if (d, s) != (0, 0)]
    for d, s in spread:
        @pl.when(exists(here + d))
        def _():
            third(d, s).start()

    parts[2, grp] = mine_part[...]
    for d, s in spread:
        @pl.when(exists(here - d))
        def _():
            third(d, s).wait_recv()

    total_mean = jnp.zeros((size, 1), F32)
    total_scale = jnp.zeros((size, 1), F32)
    total_column = jnp.zeros((size, 1), F32)
    total_back = jnp.zeros((size, width), F32)
    for r in range(3):
        for group in range(groups):
            error = jnp.zeros((1, rows), F32)
            for d in range(r - 2, r + 1):
                for sender in range(groups):
                    error = error + parts[d + 2, sender, r - d, group]
            errors[group] = error

        def backward(index, carry):
            sum_mean, sum_scale, sum_column, back = carry
            group, c = index // chunks, lax.rem(index, chunks)
            span = pl.ds(pl.multiple_of(c * LANES, LANES), LANES)
            error = errors[group, :, span]
            weight = (error * mean) * slope[r, group, :, span]
            sum_mean = sum_mean + error * value[r, group, :, span]
            sum_scale = sum_scale + weight * dist[r, group, :, span]
            sum_column = sum_column + weight
            back = back + jnp.dot(
                weight.astype(BF16), feats[r, group, span, :], preferred_element_type=F32
            )
            return sum_mean, sum_scale, sum_column, back

        flat = jnp.zeros((size, LANES), F32)
        carry = (flat, flat, flat, jnp.zeros((size, width), F32))
        if groups * chunks <= 4:
            for index in range(groups * chunks):
                carry = backward(jnp.int32(index), carry)
        else:
            carry = lax.fori_loop(0, groups * chunks, backward, carry)
        total_mean += times[r] * jnp.sum(carry[0], axis=1, keepdims=True)
        total_scale += times[r] * jnp.sum(carry[1], axis=1, keepdims=True)
        total_column += times[r] * jnp.sum(carry[2], axis=1, keepdims=True)
        total_back += times[r] * carry[3]

    norm = 1.0 / math.sqrt(rows * groups)
    grad_rows[...] = (scale * (norm / width)) * (own_f * total_column - total_back)
    for b in range(mine):
        at = slice(b * BS, (b + 1) * BS)
        grad_means[:, at] = to_row(total_mean[at]) * norm
        grad_scales[:, at] = to_row(total_scale[at]) * (norm / (2.0 * width))

    repeat(tiles - 1, lambda step: first(step).wait_send())
    for s in range(1, groups):
        for k in range(2):
            across(s, k).wait_send()

    @pl.when(exists(here + near))
    def _():
        for s in range(groups):
            for k in range(2):
                near_copy(s, k).wait_send()

    @pl.when(exists(here - near))
    def _():
        for s in range(groups):
            for k in range(2):
                far_copy(s, k).wait_send()

    for d, s in spread:
        @pl.when(exists(here + d))
        def _():
            third(d, s).wait_send()


def finish(rows, means, scales, out_rows, out_means, out_scales, sems):
    copies = [
        pltpu.make_async_copy(source, target, sems.at[index])
        for index, (source, target) in enumerate(
            ((rows, out_rows), (means, out_means), (scales, out_scales))
        )
    ]
    for copy in copies:
        copy.start()
    for copy in copies:
        copy.wait()


def shards(points, targets, morton, inducing, means, scales, neighbours):
    tiles = lax.axis_size("tile")
    groups = lax.axis_size("grp")
    rows, width = points.shape
    per = rows // tiles
    owned = inducing.shape[0] // BS
    size = owned // groups * BS
    vmem = pl.BlockSpec(memory_space=pltpu.VMEM)
    dma = pltpu.SemaphoreType.DMA
    pair = (3, groups, size, rows)
    result = pl.pallas_call(
        functools.partial(kernel, tiles, groups),
        out_shape=(
            pltpu.VMEM((size, width), F32),
            pltpu.VMEM((1, size), F32),
            pltpu.VMEM((1, size), F32),
        ),
        in_specs=[pl.BlockSpec(memory_space=pltpu.HBM)] * 7,
        out_specs=(vmem, vmem, vmem),
        scratch_shapes=[
            pltpu.VMEM((rows, width), BF16),
            pltpu.VMEM((1, rows), BF16),
            pltpu.VMEM((1, rows), jnp.int32),
            pltpu.VMEM((size, width), BF16),
            pltpu.VMEM((owned, BS), BF16),
            pltpu.VMEM((owned, BS), BF16),
            pltpu.SMEM(neighbours.shape[::-1], jnp.int32),
            dma((7,)),
            pltpu.VMEM((tiles, per, width + LANES), BF16),
            pltpu.VMEM((tiles, per, width + LANES), BF16),
            pltpu.VMEM((3, groups, rows, width), BF16),
            pltpu.VMEM((3, groups, 1, rows), F32),
            pltpu.VMEM((5, groups, 3, groups, 1, rows), F32),
            pltpu.VMEM(pair, F32),
            pltpu.VMEM(pair, F32),
            pltpu.VMEM(pair, F32),
            pltpu.VMEM((groups, 1, rows), F32),
            dma((tiles - 1,)), dma((tiles - 1,)),
            dma((3, groups, 2)), dma((3, groups, 2)),
            dma((5, groups)), dma((5, groups)),
        ],
        compiler_params=pltpu.CompilerParams(
            collective_id=0, has_side_effects=True, vmem_limit_bytes=62 << 20
        ),
    )(
        points, targets.reshape(1, rows), morton.reshape(1, rows), inducing,
        means.reshape(owned, BS), scales.reshape(owned, BS), neighbours.T,
    )
    result = pl.pallas_call(
        finish,
        out_shape=[jax.ShapeDtypeStruct(part.shape, F32) for part in result],
        in_specs=[vmem] * 3,
        out_specs=[pl.BlockSpec(memory_space=pl.ANY)] * 3,
        scratch_shapes=[dma((3,))],
        compiler_params=pltpu.CompilerParams(vmem_limit_bytes=4 << 20),
    )(*result)
    return result[0], result[1].reshape(size), result[2].reshape(size)


def solution(mesh):
    placed = (
        P(("tile", "grp"), None),
        P(("tile", "grp")),
        P(("tile", "grp")),
        P("tile", None),
        P("tile"),
        P("tile"),
        P(),
    )
    return jax.shard_map(
        shards,
        mesh=mesh,
        in_specs=placed,
        out_specs=(P(("tile", "grp"), None), P(("tile", "grp")), P(("tile", "grp"))),
        check_vma=False,
    )
```

```python
import functools
import math

import jax
import jax.numpy as jnp
from jax import lax
from jax.experimental import pallas as pl
from jax.experimental.pallas import tpu as pltpu
from jax.sharding import PartitionSpec as P

BS = 128
LANES = 128
F32 = jnp.float32
BF16 = jnp.bfloat16
MESH = pl.DeviceIdType.MESH
NT = (((1,), (1,)), ((), ()))


def iota(shape, dim):
    return lax.broadcasted_iota(jnp.int32, shape, dim)


def repeat(count, body):
    if count <= 16:
        for index in range(count):
            body(index)
    else:
        lax.fori_loop(0, count, lambda index, carry: (body(index), carry)[1], 0)


def to_column(row):
    eye = iota((LANES, LANES), 0) == iota((LANES, LANES), 1)
    return jnp.sum(jnp.where(eye, row, 0.0), axis=1, keepdims=True)


def to_row(column):
    eye = iota((LANES, LANES), 0) == iota((LANES, LANES), 1)
    return jnp.sum(jnp.where(eye, column, 0.0), axis=0, keepdims=True)


def kernel(
    tiles, groups,
    points_in, targets_in, morton_in, inducing_in, means_in, scales_in, neighbours_in,
    grad_rows, grad_means, grad_scales,
    points, targets, morton, inducing, means, scales, neighbours, loads,
    grouped, landed, feats, mine_part, parts, dist, value, slope, errors,
    send1, recv1, send2, recv2, send3, recv3,
):
    rows, width = points.shape
    per = rows // tiles
    owned = means.shape[0]
    mine = owned // groups
    size = mine * BS
    count = neighbours.shape[0]
    chunks = rows // LANES
    here = lax.axis_index("tile")
    grp = lax.axis_index("grp")

    own_rows = pl.ds(pl.multiple_of(grp * size, size), size)
    pairs = (
        (morton_in, morton), (points_in, points), (targets_in, targets),
        (inducing_in.at[own_rows, :], inducing), (means_in, means),
        (scales_in, scales), (neighbours_in, neighbours),
    )
    load = [
        pltpu.make_async_copy(pair[0], pair[1], loads.at[index])
        for index, pair in enumerate(pairs)
    ]
    for copy in load[:2]:
        copy.start()

    def exists(tile):
        return (tile >= 0) & (tile < tiles)

    def other(step):
        return lax.rem(grp + step, groups)

    def source(step):
        return lax.rem(grp + groups - step, groups)

    barrier = pltpu.get_barrier_semaphore()

    def greet(step):
        pl.semaphore_signal(
            barrier, inc=1,
            device_id=(lax.rem(here + step + 1, tiles), grp), device_id_type=MESH,
        )

    repeat(tiles - 1, greet)
    for copy in load[2:]:
        copy.start()
    expected = jnp.int32(tiles - 1)
    for d in range(-2, 3):
        there = exists(here + d)
        expected += jnp.where(there, groups - 1, 0)

        @pl.when(there)
        def _():
            for step in range(1, groups):
                pl.semaphore_signal(
                    barrier, inc=1, device_id=(here + d, other(step)), device_id_type=MESH
                )

        if d:
            @pl.when(jnp.logical_not(there))
            def _():
                parts[d + 2] = jnp.zeros(parts.shape[1:], F32)
                if abs(d) == 1:
                    feats[d + 1] = jnp.zeros(feats.shape[1:], BF16)

    for copy in load[:3]:
        copy.wait()

    codes = morton[...]
    member = iota((tiles, rows), 0) == codes
    before = jnp.dot(
        member.astype(F32).astype(BF16),
        (iota((rows, rows), 0) < iota((rows, rows), 1)).astype(F32).astype(BF16),
        preferred_element_type=F32,
    )
    rank = jnp.sum(jnp.where(member, before, 0.0), axis=0, keepdims=True)
    place = codes * per + rank.astype(jnp.int32)
    chosen = iota((rows, rows), 0) == place
    moved = jnp.dot(
        chosen.astype(F32).astype(BF16), points[...], preferred_element_type=F32
    )
    goals = jnp.sum(jnp.where(chosen, targets[...].astype(F32), 0.0), axis=1, keepdims=True)
    grouped[:, :, :width] = moved.reshape(tiles, per, width).astype(BF16)
    grouped[:, :, width:] = (
        jnp.broadcast_to(goals, (rows, LANES)).reshape(tiles, per, LANES).astype(BF16)
    )
    pl.semaphore_wait(barrier, expected)

    def first(step):
        to = lax.rem(here + step + 1, tiles)
        return pltpu.make_async_remote_copy(
            src_ref=grouped.at[to], dst_ref=landed.at[here],
            send_sem=send1.at[step], recv_sem=recv1.at[step],
            device_id=(to, grp), device_id_type=MESH,
        )

    repeat(tiles - 1, lambda step: first(step).start())
    landed[here] = grouped[here]

    for copy in load[3:]:
        copy.wait()
    own = inducing[...]
    own_f = own.astype(F32)
    own_sq = jnp.sum(own_f * own_f, axis=1, keepdims=True)

    def own_column(ref):
        every = ref[...].astype(F32)
        picked = [
            to_column(jnp.sum(
                jnp.where(iota(every.shape, 0) == grp * mine + b, every, 0.0),
                axis=0, keepdims=True,
            ))
            for b in range(mine)
        ]
        return jnp.concatenate(picked, axis=0)

    mean = own_column(means)
    scale = own_column(scales)
    scaled = scale / (2.0 * width)
    times = []
    for r in range(3):
        tile = here + r - 1
        row = jnp.clip(tile, 0, tiles - 1)
        pieces = []
        for b in range(mine):
            block = here * owned + grp * mine + b
            listed = jnp.int32(0)
            for k in range(count):
                listed += jnp.where(neighbours[k, row] == block, 1, 0)
            listed = jnp.where(exists(tile), listed, 0)
            pieces.append(jnp.full((BS, 1), listed.astype(F32), F32))
        times.append(jnp.concatenate(pieces, axis=0))

    near = 1 - 2 * lax.rem(here, 2)

    half = tiles // 2
    front = here // half

    def part(k):
        return front if k == 0 else 1 - front

    def share(d, step, group, to, k):
        span = pl.ds(pl.multiple_of(part(k) * (rows // 2), rows // 2), rows // 2)
        return pltpu.make_async_remote_copy(
            src_ref=feats.at[1, group, span, :], dst_ref=feats.at[1 - d, group, span, :],
            send_sem=send2.at[1 - d, step, k], recv_sem=recv2.at[1 - d, step, k],
            device_id=(here + d, to), device_id_type=MESH,
        )

    def across(step, k):
        return share(0, step, grp, other(step), k)

    def far_copy(step, k):
        return share(-near, step, grp, other(step), k)

    def near_copy(step, k):
        return share(near, step, source(step), grp, k)

    for k in range(2):
        def landing(index):
            tile = part(k) * half + index

            @pl.when(tile != here)
            def _():
                first(lax.rem(here - tile - 1 + tiles, tiles)).wait_recv()

        repeat(half, landing)
        mine_half = landed[pl.ds(part(k) * half, half), :, :].astype(F32)
        mine_half = mine_half.reshape(rows // 2, width + LANES)
        span = pl.ds(pl.multiple_of(part(k) * (rows // 2), rows // 2), rows // 2)
        feats[1, grp, span, :] = mine_half[:, :width].astype(BF16)

        for s in range(1, groups):
            across(s, k).start()

        @pl.when(exists(here + near))
        def _():
            near_copy(0, k).start()

        @pl.when(exists(here - near))
        def _():
            for s in range(groups):
                far_copy(s, k).start()

    arrived = landed[:, :, width:].astype(F32).reshape(rows, LANES)
    ones = jnp.ones((8, width), BF16)

    def forward(r, group, listed):
        def piece(c):
            span = pl.ds(pl.multiple_of(c * LANES, LANES), LANES)
            block = feats[r, group, span, :]
            block_f = block.astype(F32)
            square = block_f * block_f
            high = square.astype(BF16)
            low = (square - high.astype(F32)).astype(BF16)
            feat_sq = (
                lax.dot_general(ones, high, NT, preferred_element_type=F32)
                + lax.dot_general(ones, low, NT, preferred_element_type=F32)
            )[:1]
            cross = lax.dot_general(own, block, NT, preferred_element_type=F32)
            far = (feat_sq + own_sq) - 2.0 * cross
            radius = jnp.sqrt(jnp.maximum(scaled * far, 0.0))
            remain = 1.0 - jnp.minimum(radius, 1.0)
            square_r = remain * remain
            height = square_r * square_r * (4.0 * radius + 1.0)
            dist[r, group, :, span] = far
            value[r, group, :, span] = height
            slope[r, group, :, span] = -10.0 * (square_r * remain)
            mine_part[r, group, :, span] = jnp.sum(
                (mean * listed) * height, axis=0, keepdims=True
            )

        repeat(chunks, piece)

    def third(r, e, step):
        d = r - 1 + e
        return pltpu.make_async_remote_copy(
            src_ref=mine_part.at[r], dst_ref=parts.at[2 - d, grp, r],
            send_sem=send3.at[r, e + 1, step], recv_sem=recv3.at[r, e + 1, step],
            device_id=(here + d, other(step)), device_id_type=MESH,
        )

    def publish(r):
        for e in (1, -1, 0):
            for step in range(groups):
                d = r - 1 + e

                @pl.when(exists(here + d) & ((d != 0) | (step != 0)))
                def _():
                    third(r, e, step).start()

    spread = [
        (r, e, s) for r in range(3) for e in range(-1, 2) for s in range(groups)
        if (r - 1 + e, s) != (0, 0)
    ]
    forward(1, grp, times[1])
    for c in range(chunks):
        span = pl.ds(c * LANES, LANES)
        goal = to_row(arrived[c * LANES:(c + 1) * LANES])
        mine_part[1, grp, :, span] = mine_part[1, grp, :, span] - goal

    for s in range(1, groups):
        for k in range(2):
            across(s, k).wait_recv()

            @pl.when(exists(here + near))
            def _():
                near_copy(s, k).start()

        forward(1, source(s), times[1])

    publish(jnp.int32(1))
    for side in (near, -near):
        listed = jnp.where(side > 0, times[2], times[0])
        for s in range(groups):
            @pl.when(exists(here + side))
            def _():
                for k in range(2):
                    share(-side, s, source(s), grp, k).wait_recv()

            forward(1 + side, source(s), listed)
        publish(1 + side)

    parts[2, grp] = mine_part[...]
    for r, e, s in spread:
        @pl.when(exists(here - (r - 1 + e)))
        def _():
            third(r, e, s).wait_recv()

    total_mean = jnp.zeros((size, 1), F32)
    total_scale = jnp.zeros((size, 1), F32)
    total_column = jnp.zeros((size, 1), F32)
    total_back = jnp.zeros((size, width), F32)
    for r in range(3):
        for group in range(groups):
            error = jnp.zeros((1, rows), F32)
            for d in range(r - 2, r + 1):
                for sender in range(groups):
                    error = error + parts[d + 2, sender, r - d, group]
            errors[group] = error

        def backward(index, carry):
            sum_mean, sum_scale, sum_column, back = carry
            group, c = index // chunks, lax.rem(index, chunks)
            span = pl.ds(pl.multiple_of(c * LANES, LANES), LANES)
            error = errors[group, :, span]
            weight = (error * mean) * slope[r, group, :, span]
            sum_mean = sum_mean + error * value[r, group, :, span]
            sum_scale = sum_scale + weight * dist[r, group, :, span]
            sum_column = sum_column + weight
            back = back + jnp.dot(
                weight.astype(BF16), feats[r, group, span, :], preferred_element_type=F32
            )
            return sum_mean, sum_scale, sum_column, back

        flat = jnp.zeros((size, LANES), F32)
        carry = (flat, flat, flat, jnp.zeros((size, width), F32))
        if groups * chunks <= 4:
            for index in range(groups * chunks):
                carry = backward(jnp.int32(index), carry)
        else:
            carry = lax.fori_loop(0, groups * chunks, backward, carry)
        total_mean += times[r] * jnp.sum(carry[0], axis=1, keepdims=True)
        total_scale += times[r] * jnp.sum(carry[1], axis=1, keepdims=True)
        total_column += times[r] * jnp.sum(carry[2], axis=1, keepdims=True)
        total_back += times[r] * carry[3]

    norm = 1.0 / math.sqrt(rows * groups)
    grad_rows[...] = (scale * (norm / width)) * (own_f * total_column - total_back)
    for b in range(mine):
        at = slice(b * BS, (b + 1) * BS)
        grad_means[:, at] = to_row(total_mean[at]) * norm
        grad_scales[:, at] = to_row(total_scale[at]) * (norm / (2.0 * width))

    repeat(tiles - 1, lambda step: first(step).wait_send())
    for s in range(1, groups):
        for k in range(2):
            across(s, k).wait_send()

    @pl.when(exists(here + near))
    def _():
        for s in range(groups):
            for k in range(2):
                near_copy(s, k).wait_send()

    @pl.when(exists(here - near))
    def _():
        for s in range(groups):
            for k in range(2):
                far_copy(s, k).wait_send()

    for r, e, s in spread:
        @pl.when(exists(here + (r - 1 + e)))
        def _():
            third(r, e, s).wait_send()


def finish(rows, means, scales, out_rows, out_means, out_scales, sems):
    copies = [
        pltpu.make_async_copy(source, target, sems.at[index])
        for index, (source, target) in enumerate(
            ((rows, out_rows), (means, out_means), (scales, out_scales))
        )
    ]
    for copy in copies:
        copy.start()
    for copy in copies:
        copy.wait()


def shards(points, targets, morton, inducing, means, scales, neighbours):
    tiles = lax.axis_size("tile")
    groups = lax.axis_size("grp")
    rows, width = points.shape
    per = rows // tiles
    owned = inducing.shape[0] // BS
    size = owned // groups * BS
    vmem = pl.BlockSpec(memory_space=pltpu.VMEM)
    dma = pltpu.SemaphoreType.DMA
    pair = (3, groups, size, rows)
    result = pl.pallas_call(
        functools.partial(kernel, tiles, groups),
        out_shape=(
            pltpu.VMEM((size, width), F32),
            pltpu.VMEM((1, size), F32),
            pltpu.VMEM((1, size), F32),
        ),
        in_specs=[pl.BlockSpec(memory_space=pltpu.HBM)] * 7,
        out_specs=(vmem, vmem, vmem),
        scratch_shapes=[
            pltpu.VMEM((rows, width), BF16),
            pltpu.VMEM((1, rows), BF16),
            pltpu.VMEM((1, rows), jnp.int32),
            pltpu.VMEM((size, width), BF16),
            pltpu.VMEM((owned, BS), BF16),
            pltpu.VMEM((owned, BS), BF16),
            pltpu.SMEM(neighbours.shape[::-1], jnp.int32),
            dma((7,)),
            pltpu.VMEM((tiles, per, width + LANES), BF16),
            pltpu.VMEM((tiles, per, width + LANES), BF16),
            pltpu.VMEM((3, groups, rows, width), BF16),
            pltpu.VMEM((3, groups, 1, rows), F32),
            pltpu.VMEM((5, groups, 3, groups, 1, rows), F32),
            pltpu.VMEM(pair, F32),
            pltpu.VMEM(pair, F32),
            pltpu.VMEM(pair, F32),
            pltpu.VMEM((groups, 1, rows), F32),
            dma((tiles - 1,)), dma((tiles - 1,)),
            dma((3, groups, 2)), dma((3, groups, 2)),
            dma((3, 3, groups)), dma((3, 3, groups)),
        ],
        compiler_params=pltpu.CompilerParams(
            collective_id=0, has_side_effects=True, vmem_limit_bytes=62 << 20
        ),
    )(
        points, targets.reshape(1, rows), morton.reshape(1, rows), inducing,
        means.reshape(owned, BS), scales.reshape(owned, BS), neighbours.T,
    )
    result = pl.pallas_call(
        finish,
        out_shape=[jax.ShapeDtypeStruct(part.shape, F32) for part in result],
        in_specs=[vmem] * 3,
        out_specs=[pl.BlockSpec(memory_space=pl.ANY)] * 3,
        scratch_shapes=[dma((3,))],
        compiler_params=pltpu.CompilerParams(vmem_limit_bytes=4 << 20),
    )(*result)
    return result[0], result[1].reshape(size), result[2].reshape(size)


def solution(mesh):
    placed = (
        P(("tile", "grp"), None),
        P(("tile", "grp")),
        P(("tile", "grp")),
        P("tile", None),
        P("tile"),
        P("tile"),
        P(),
    )
    return jax.shard_map(
        shards,
        mesh=mesh,
        in_specs=placed,
        out_specs=(P(("tile", "grp"), None), P(("tile", "grp")), P(("tile", "grp"))),
        check_vma=False,
    )
```
